512 devices in a mesh: expert: 8 (over y), dp: 8 (over x, core), shard: 8 (over z).
Axes of the slice: x: 4, y: 8, z: 8, core: 2. Of those that a mesh axis runs over, the one named last changes fastest.
Arguments:
- grad_partials: bfloat16 [8, 8, 4096, 1536], P('dp', 'expert', 'shard'), may hold values from -120 to 120
- momentum: float32 [8, 8, 512, 1536], P('expert', 'shard', 'dp'), may hold values from -3 to 3
- q_factor: float32 [1536, 8, 384], P(('dp', 'shard'), 'expert'), may hold values from -0.15625 to 0.15625
Outputs:
- next_momentum: float32 [8, 8, 512, 1536], P('expert', 'shard', 'dp')
- next_factor: float32 [1536, 8, 384], P(('dp', 'shard'), 'expert')
- weight_update: bfloat16 [8, 4096, 1536], P('expert', 'shard')
The draws below stay inside these ranges and needn't reach their ends.
All inputs are finite; a program needn't handle non-finite values.
Results may differ from the reference program's by a relative error of at most 0.015.
Values may be sent and summed in bfloat16 or wider, within the bound.
No kernel may reach another device: no remote copies, remote signals or barrier semaphores. Data moves between devices by JAX's collectives and lax.ppermute only.
A program may use at most 64 MiB of HBM per device.

```python
import math
import jax
import jax.numpy as jnp
from jax import lax

D = 4096
FF = 1536
R = 384
EXPERTS = 8
SHARD_ROWS = 512
N_DP = 8
N_SHARD = 8


def draw_grad_partials(key, part):
    subkeys = jax.random.split(key, 3)
    log_span = math.log(10.0)
    row_scale = jnp.exp(jax.random.uniform(subkeys[0], (1, EXPERTS, D, 1), jnp.float32, 0.0, log_span))
    column_scale = jnp.exp(jax.random.uniform(subkeys[1], (1, EXPERTS, 1, FF), jnp.float32, 0.0, log_span))
    expert_place = jnp.arange(EXPERTS, dtype=jnp.float32).reshape(1, EXPERTS, 1, 1) / max(EXPERTS - 1, 1)
    row_place = jnp.arange(D, dtype=jnp.float32).reshape(1, 1, D, 1) / (D - 1)
    growth = jnp.exp(math.log(3.0) * 0.5 * (expert_place + row_place))
    entries = jnp.clip(jax.random.normal(subkeys[2], (N_DP, EXPERTS, D, FF), jnp.float32), -4.0, 4.0)
    return (0.1 * entries * row_scale * column_scale * growth).astype(jnp.bfloat16)


def shard_levels(key, extent, shards, smallest, high):
    def one(position, shards_of):
        draws = jax.random.uniform(jax.random.fold_in(jax.random.fold_in(key, 6), position), (shards_of,), jnp.float32, smallest / len(shards), high / len(shards))
        return jnp.repeat(jnp.exp(draws), extent[position] // shards_of).reshape((-1,) + (1,) * (len(extent) - position - 1))

    level = one(*shards[0])
    for cut in shards[1:]:
        level = level * one(*cut)
    return level


def centred(rng, extent, width, bound, shards=(), held_as=jnp.bfloat16):
    values = jax.random.normal(rng, extent, jnp.float32) * width
    if len(shards) > 0:
        values = shard_levels(rng, extent, shards, -0.22, 0.18) * values
    return jnp.clip(values, min=-bound, max=bound).astype(held_as)


def setup_inputs(seed: int = 0) -> dict:
    key_list = jax.random.split(jax.random.key(seed), 4)
    return {
        "grad_partials": draw_grad_partials(jax.random.fold_in(key_list[3], 71), 0),
        "momentum": centred(key_list[1], (EXPERTS, N_SHARD, SHARD_ROWS, FF), 0.5, 3.0, ((0, 8), (1, 8), (2, 8)), jnp.float32),
        "q_factor": centred(key_list[2], (FF, EXPERTS, R), FF ** -0.5, 0.15625, ((0, 64), (1, 8)), jnp.float32),
    }


clip_rms = 0.5
keep_share = 0.95
highest = lax.Precision.HIGHEST

def reference(grad_partials, momentum, q_factor):
    gradient = grad_partials[0].astype(jnp.float32)
    for replica in range(1, N_DP):
        gradient = gradient + grad_partials[replica].astype(jnp.float32)
    square_sum = jnp.sum(gradient * gradient)
    clip_scale = clip_rms / jnp.sqrt(square_sum / gradient.size + 1e-06)
    experts = gradient.shape[0]
    buffer = momentum.reshape(experts, D, FF) + clip_scale * gradient
    unit_scale = math.sqrt(D * FF / R)

    def per_expert(operands):
        buffer_one, factor_one = operands
        projected = jnp.dot(buffer_one, factor_one, precision=highest)
        gram_matrix = jnp.dot(projected.T, projected, precision=highest)
        triangle = jnp.linalg.cholesky(gram_matrix)
        ortho_basis = jax.scipy.linalg.solve_triangular(triangle, projected.T, lower=True).T
        right_factor = jnp.dot(buffer_one.T, ortho_basis, precision=highest)
        inverse = lax.rsqrt(lax.optimization_barrier(jnp.sum(right_factor * right_factor, axis=0)) + 1e-06)
        next_factor = right_factor * inverse
        correction = jnp.dot(ortho_basis, right_factor.T, precision=highest)
        direction = jnp.dot(ortho_basis * inverse, right_factor.T, precision=highest)
        next_momentum = buffer_one - (1.0 - keep_share) * correction
        weight_update = (unit_scale * direction).astype(jnp.bfloat16)
        return (next_momentum, next_factor, weight_update)
    next_momentum, next_factor, weight_update = lax.map(per_expert, (buffer, jnp.swapaxes(q_factor, 0, 1)))
    return (next_momentum.reshape(experts, N_SHARD, D // N_SHARD, FF), jnp.swapaxes(next_factor, 0, 1), weight_update)
```

```python
import math

import jax
import jax.numpy as jnp
from jax import lax
from jax.sharding import Mesh
from jax.sharding import PartitionSpec as P

DP_SHARD = ("dp_0", "dp_1", "shard")
DP = ("dp_0", "dp_1")


clip_rms = 0.5
keep_share = 0.95
highest = lax.Precision.HIGHEST


def exchange(blocks, axes):
    return lax.all_to_all(blocks, axes, split_axis=0, concat_axis=0, tiled=True)


def sent_to_all(x, axes):
    return exchange(jnp.broadcast_to(x, (lax.axis_size(axes), *x.shape)), axes)


def total_over(x, axes):
    return jnp.sum(sent_to_all(x, axes), axis=0)


def shards(grad_partials, momentum, q_factor):
    n_dp, n_all = lax.axis_size(DP), lax.axis_size(DP_SHARD)
    all_rows, width = grad_partials.shape[2:]
    rows = all_rows // n_dp
    factor_rows, _, rank = q_factor.shape

    q_rows = sent_to_all(q_factor[:, 0].astype(jnp.bfloat16), DP_SHARD)
    arrived = exchange(grad_partials.reshape(n_dp, rows, width), DP)
    gradient = jnp.sum(arrived.astype(jnp.float32), axis=0)
    square_sum = jnp.sum(gradient * gradient).reshape(1, 1)
    square_sum = total_over(square_sum, ("dp_1", "shard"))
    square_sum = total_over(square_sum, ("expert", "dp_0"))[0, 0]
    entries = float(lax.axis_size("expert") * n_all * rows * width)
    clip_scale = clip_rms / jnp.sqrt(square_sum / entries + 1e-06)
    buffer = momentum[0, 0] + clip_scale * gradient

    q = q_rows.reshape(n_all * factor_rows, rank).astype(jnp.float32)
    projected = jnp.dot(buffer, q, precision=highest)
    gram_part = lax.dot_general(
        projected, projected, (((0,), (0,)), ((), ())), precision=highest
    )
    right_part = lax.dot_general(
        buffer, projected, (((0,), (0,)), ((), ())), precision=highest
    ).astype(jnp.bfloat16)

    gram_rows = jnp.sum(exchange(gram_part.reshape(n_all, rank // n_all, rank), DP_SHARD), axis=0)
    gram = sent_to_all(gram_rows, DP_SHARD).reshape(rank, rank)
    raw_rows = jnp.sum(
        exchange(right_part.reshape(n_all, factor_rows, rank), DP_SHARD).astype(jnp.float32),
        axis=0,
    ).astype(jnp.bfloat16)
    raw = sent_to_all(raw_rows, DP_SHARD).reshape(width, rank).astype(jnp.float32)
    replica_rows = sent_to_all(projected, DP).reshape(all_rows, rank)

    lower = jnp.linalg.cholesky(gram)
    inverse_lower = jax.scipy.linalg.solve_triangular(
        lower, jnp.eye(rank, dtype=jnp.float32), lower=True
    )
    back = (((1,), (1,)), ((), ()))
    right = lax.dot_general(raw, inverse_lower, back, precision=highest)
    inverse = lax.rsqrt(jnp.sum(right * right, axis=0) + 1e-06)
    basis = lax.dot_general(projected, inverse_lower, back, precision=highest)
    replica_basis = lax.dot_general(replica_rows, inverse_lower, back, precision=highest)

    offset = (lax.axis_index(DP) * lax.axis_size("shard") + lax.axis_index("shard")) * factor_rows
    next_factor = lax.dynamic_slice_in_dim(right, offset, factor_rows, 0) * inverse
    correction = lax.dot_general(basis, right, back, precision=highest)
    next_momentum = buffer - (1.0 - keep_share) * correction
    unit_scale = math.sqrt(lax.axis_size("shard") * all_rows * width / rank)
    direction = lax.dot_general(replica_basis * inverse, right, back, precision=highest)
    weight_update = (unit_scale * direction).astype(jnp.bfloat16)
    return (next_momentum[None, None], next_factor[:, None], weight_update[None])


def solution(mesh):
    torus = Mesh(
        mesh.devices.reshape(mesh.shape["expert"], 4, 2, mesh.shape["shard"]),
        ("expert", "dp_0", "dp_1", "shard"),
    )
    in_specs = (
        P(DP, "expert", "shard", None),
        P("expert", "shard", DP, None),
        P(DP_SHARD, "expert", None),
    )
    out_specs = (
        P("expert", "shard", DP, None),
        P(DP_SHARD, "expert", None),
        P("expert", "shard", None),
    )
    return jax.shard_map(
        shards, mesh=torus, in_specs=in_specs, out_specs=out_specs, check_vma=False
    )
```

```python
import math

import jax
import jax.numpy as jnp
from jax import lax
from jax.experimental import pallas as pl
from jax.experimental.pallas import tpu as pltpu
from jax.sharding import Mesh
from jax.sharding import PartitionSpec as P

DP = ("dp_0", "dp_1")
CHIPS = ("dp_0", "shard")
DP_SHARD = ("dp_0", "dp_1", "shard")
CORE = "dp_1"

clip_rms = 0.5
keep_share = 0.95
highest = lax.Precision.HIGHEST
high = lax.Precision.HIGH
f32, bf16 = jnp.float32, jnp.bfloat16

SUB, LANES = 8, 128


def inverse_of_block(rows):
    lane = lax.broadcasted_iota(jnp.int32, (SUB, LANES), 1)
    sub = lax.broadcasted_iota(jnp.int32, (SUB, LANES), 0)

    def spread_lane(x, j):
        return jnp.broadcast_to(x[:, j : j + 1], (SUB, LANES))

    def spread_row(x, k):
        return jnp.broadcast_to(x[k : k + 1, :], (SUB, LANES))

    rows, done = list(rows), []
    for p in range(LANES // SUB):
        first = p * SUB
        below = rows[p:]
        columns = [[spread_lane(r, first + k) for k in range(SUB)] for r in below]
        inside = (lane >= first) & (lane < first + SUB)
        top = jnp.where(inside, jnp.where(lane - first == sub, 1.0, 0.0), below[0])
        rest = [jnp.where(inside, 0.0, r) for r in below[1:]]
        head, tails = columns[0], columns[1:]
        scale = jnp.zeros((SUB, LANES), f32)
        for k in range(SUB):
            pivot = spread_row(head[k], k)
            share = 1.0 / pivot
            scale = jnp.where(sub == k, lax.rsqrt(pivot), scale)
            line = spread_row(top, k)
            ahead = {m: spread_row(head[m], k) for m in range(k + 1, SUB)}
            factor = jnp.where(sub > k, head[k] * share, 0.0)
            top = top - factor * line
            for m in ahead:
                head[m] = head[m] - factor * ahead[m]
            for r in range(len(rest)):
                factor = tails[r][k] * share
                rest[r] = rest[r] - factor * line
                for m in ahead:
                    tails[r][m] = tails[r][m] - factor * ahead[m]
        done.append(jnp.where(lane - first <= sub, top * scale, 0.0))
        rows[p + 1 :] = rest
    return done


def dot(x, y, over):
    return lax.dot_general(
        x, y, ((over[:1], over[1:]), ((), ())), precision=highest, preferred_element_type=f32
    )


def inverse_lower_kernel(gram_ref, out_ref, left_ref):
    n = gram_ref.shape[0]
    left_ref[...] = gram_ref[...]
    for lo in range(0, n, LANES):
        hi = lo + LANES
        inv = jnp.concatenate(
            inverse_of_block([left_ref[r : r + SUB, lo:hi] for r in range(lo, hi, SUB)]), axis=0
        )
        out_ref[lo:hi, lo:hi] = inv
        if lo > 0:
            out_ref[lo:hi, :lo] = dot(inv, left_ref[lo:hi, :lo], (1, 0))
        if hi < n:
            out_ref[lo:hi, hi:] = jnp.zeros((LANES, n - hi), f32)
            right = dot(inv, left_ref[lo:hi, hi:], (1, 0))
            left_ref[hi:, hi:] = left_ref[hi:, hi:] - dot(right, right, (0, 0))
            new = dot(right, out_ref[lo:hi, :hi], (0, 0))
            if lo > 0:
                left_ref[hi:, :lo] = left_ref[hi:, :lo] - new[:, :lo]
            left_ref[hi:, lo:hi] = -new[:, lo:]


def inverse_lower(gram):
    n = gram.shape[0]
    vmem = pl.BlockSpec(memory_space=pltpu.VMEM)
    return pl.pallas_call(
        inverse_lower_kernel,
        out_shape=jax.ShapeDtypeStruct((n, n), f32),
        in_specs=[vmem],
        out_specs=vmem,
        scratch_shapes=[pltpu.VMEM((n, n), f32)],
        compiler_params=pltpu.CompilerParams(vmem_limit_bytes=24 << 20),
        cost_estimate=pl.CostEstimate(
            flops=10**10, bytes_accessed=8 * n * n, transcendentals=0
        ),
    )(gram)


def exchange(blocks, axes):
    return lax.all_to_all(blocks, axes, split_axis=0, concat_axis=0, tiled=True)


def sent_to_all(x, axes):
    return exchange(jnp.broadcast_to(x, (lax.axis_size(axes), *x.shape)), axes)


def total_over(x, axes):
    return jnp.sum(sent_to_all(x, axes), axis=0)


def other_core(x):
    return lax.ppermute(x, CORE, [(0, 1), (1, 0)])


def two_pieces(x):
    large = x.astype(bf16)
    return large, (x - large.astype(f32)).astype(bf16)


def shards(grad_partials, momentum, q_factor):
    n_dp, n_shard, n_chips = (lax.axis_size(a) for a in (DP, "shard", CHIPS))
    all_rows, width = grad_partials.shape[2:]
    rows, half = all_rows // n_dp, width // 2
    factor_rows, _, rank = q_factor.shape
    core = lax.axis_index(CORE)

    q_near = sent_to_all(q_factor[:, 0].astype(bf16), DP)
    partials, q_near = lax.optimization_barrier((grad_partials, q_near))
    q_all = lax.all_gather(q_near.reshape(n_dp * factor_rows, rank), "shard", axis=0, tiled=True)
    q = jnp.swapaxes(q_all.reshape(n_shard, n_dp, factor_rows, rank), 0, 1).reshape(width, rank)

    arrived = exchange(partials.reshape(n_dp, rows, width), DP)
    gradient = jnp.sum(arrived.astype(f32), axis=0)
    square_sum = total_over(jnp.sum(gradient * gradient).reshape(1, 1), DP)
    square_sum = total_over(square_sum, ("expert", "shard"))[0, 0]
    entries = float(lax.axis_size("expert") * n_chips * 2 * rows * width)
    clip_scale = clip_rms / jnp.sqrt(square_sum / entries + 1e-06)

    momentum_rows = momentum[0, 0]
    chip_gradient = jnp.concatenate([gradient, other_core(gradient)], axis=0)
    chip_momentum = jnp.concatenate([momentum_rows, other_core(momentum_rows)], axis=0)
    buffer = chip_momentum + clip_scale * chip_gradient
    projected = jnp.dot(buffer, q.astype(f32), precision=highest)

    spare = jnp.zeros((rows // 2, rank), f32)
    wide_rows = jnp.concatenate([projected[:rows], spare], axis=0)
    replica_rows = lax.all_gather(wide_rows, DP, axis=0, tiled=True)
    replica_rows = replica_rows.reshape(n_dp, -1, rank)[:, :rows].reshape(all_rows, rank)

    third = rank // 3
    own_columns = lax.dynamic_slice_in_dim(buffer, core * half, half, 1)
    raw_part = dot(own_columns, projected, (0, 0)).astype(bf16)
    one, two, three = (projected[:, i * third : (i + 1) * third] for i in range(3))
    upper = jnp.concatenate([dot(one, projected[:, : 2 * third], (0, 0)), dot(two, two, (0, 0))], axis=1)
    lower = dot(three, projected, (0, 0))
    gram_part = jnp.where(core == 0, upper, lower)
    pieces = [raw_part, *two_pieces(gram_part)]
    packed = jnp.concatenate([x.reshape(n_chips, -1, rank) for x in pieces], axis=1)
    summed = jnp.sum(exchange(packed, CHIPS).astype(f32), axis=0)
    gram_rows = (summed.shape[0] - factor_rows) // 2
    raw_rows, large, small = jnp.split(summed, [factor_rows, factor_rows + gram_rows])

    gram_all = sent_to_all(large + small, DP_SHARD)
    gram_halves = jnp.swapaxes(
        gram_all.reshape(n_dp // 2, 2, n_shard, gram_rows, rank), 0, 1
    ).reshape(2, third, rank)
    first, last = gram_halves
    middle = jnp.concatenate(
        [first[:, third : 2 * third].T, first[:, 2 * third :], last[:, third : 2 * third].T], axis=1
    )
    gram = jnp.concatenate(
        [jnp.concatenate([first[:, : 2 * third], last[:, :third].T], axis=1), middle, last], axis=0
    )
    raw_rows, gram = lax.optimization_barrier((raw_rows.astype(bf16), gram))
    own_half = sent_to_all(raw_rows, CHIPS).reshape(half, rank)
    inv_lower = inverse_lower(gram)
    own_half, inv_lower = lax.optimization_barrier((own_half, inv_lower))
    other_half = other_core(own_half)

    back = (((1,), (1,)), ((), ()))
    own_right, other_right = (
        lax.dot_general(x.astype(f32), inv_lower, back, precision=high)
        for x in (own_half, other_half)
    )
    right = jnp.concatenate(
        [
            jnp.where(core == 0, own_right, other_right),
            jnp.where(core == 0, other_right, own_right),
        ],
        axis=0,
    )
    inverse = lax.rsqrt(jnp.sum(right * right, axis=0) + 1e-06)
    replica_basis = lax.dot_general(replica_rows, inv_lower, back, precision=high)
    basis = lax.dot_general(projected[:rows], inv_lower, back, precision=high)

    offset = (lax.axis_index(DP) * n_shard + lax.axis_index("shard")) * factor_rows
    next_factor = lax.dynamic_slice_in_dim(right, offset, factor_rows, 0) * inverse
    correction = lax.dot_general(basis, right, back, precision=high)
    next_momentum = buffer[:rows] - (1.0 - keep_share) * correction
    unit_scale = math.sqrt(n_shard * all_rows * width / rank)
    direction = lax.dot_general(replica_basis * (unit_scale * inverse), right, back, precision=high)
    return (next_momentum[None, None], next_factor[:, None], direction.astype(bf16)[None])


def solution(mesh):
    torus = Mesh(
        mesh.devices.reshape(mesh.shape["expert"], 4, 2, mesh.shape["shard"]),
        ("expert", "dp_0", "dp_1", "shard"),
    )
    in_specs = (
        P(DP, "expert", "shard", None),
        P("expert", "shard", DP, None),
        P(DP_SHARD, "expert", None),
    )
    out_specs = (
        P("expert", "shard", DP, None),
        P(DP_SHARD, "expert", None),
        P("expert", "shard", None),
    )
    return jax.shard_map(
        shards, mesh=torus, in_specs=in_specs, out_specs=out_specs, check_vma=False
    )
```
